32 devices in a mesh: groups: 2 (over y), space: 4 (over z), src: 4 (over x, core).
Axes of the slice: x: 2, y: 2, z: 4, core: 2. Of those that a mesh axis runs over, the one named last changes fastest.
Arguments:
- conductivity: float32 [32, 64, 256], P(('groups', 'space')), parts along dimension 0, may hold values from 0.2 to 5
- inverse_coefficients: float32 [27, 32, 64, 256], P(None, ('groups', 'space')), parts along dimension 1
- forward_potential: float32 [16, 16, 64, 256], P(('groups', 'src'), 'space'), parts along dimension 0, may hold values from -6 to 6
- misfit_field: float32 [16, 16, 64, 256], P(('groups', 'src'), 'space'), parts along dimension 0
- electrodes: int32 [16, 2], P(('groups', 'src')), parts along dimension 0, may hold values from 0 to 262143
- assignment: int32 [16], P(('groups', 'src')), parts along dimension 0, may hold values from 0 to 3
- line_weight: float32 [8], P('groups'), parts along dimension 0, may hold values from 0.5 to 2
Outputs:
- adjoint_field: float32 [16, 16, 64, 256], P(('groups', 'src'), 'space'), parts along dimension 0
- gradient: float32 [32, 64, 256], P(('groups', 'space'), 'src'), parts along dimension 0
The draws below stay inside these ranges and needn't reach their ends.
There are 2 independent parts, one for each index of `groups`. The reference program is written for one: setup_inputs(seed, part) draws one part's arguments, and reference() takes and returns one part's arrays. A program takes and returns all parts, laid end to end along the dimension named above; each array names one. Nothing has to cross between parts.
All inputs are finite; a program needn't handle non-finite values.
Results may differ from the reference program's by a relative error of at most 0.0001.
Values sent between devices are 32-bit elements; how exact they have to be, the bound alone decides.
A program may use at most 128 MiB of HBM per device.

```python
import math
import jax
import jax.numpy as jnp

NY = 64
NZ = 256
ITERS = 2
LINES = 4
NX = 16
SOURCES = 8


def draw_misfit_field(key, part):
    key = jax.random.fold_in(key, 11)
    rising = 1.0 + 2.0 * jnp.arange(NX, dtype=jnp.float32) / (NX - 1)
    rising = rising[None, :, None, None]
    full_shape = (SOURCES, NX, NY, NZ)
    return jax.random.normal(key, full_shape, jnp.float32) * rising


def draw_inverse_coefficients(key, part):
    key = jax.random.fold_in(key, 23)
    center_key, side_key = jax.random.split(key)
    side_terms = jax.random.uniform(side_key, (27, NX, NY, NZ), jnp.float32, -0.015, 0.015)
    top_value = 2.0
    centers = jnp.exp(jax.random.uniform(center_key, (NX, NY, NZ), jnp.float32, math.log(0.5), math.log(top_value)))
    selector = (jnp.arange(27) == 13)[:, None, None, None]
    return jnp.where(selector, centers[None], side_terms)


def plant(entries, own_key, smallest, high):
    longest = entries.shape.index(max(entries.shape))
    spots = []
    for shift in (0, 1):
        where = [jax.random.randint(jax.random.fold_in(own_key, axis), (), 0, length) for axis, length in enumerate(entries.shape)]
        where[longest] = (where[longest] + shift) % entries.shape[longest]
        spots.append(tuple(where))
    return entries.at[spots[0]].set(smallest).at[spots[1]].set(high)


def levels(own_key, shape, cuts, smallest, high):
    loudness = 1.0
    for dim, blocks in cuts:
        steps = jax.random.uniform(jax.random.fold_in(jax.random.fold_in(own_key, 6), dim), (blocks,), jnp.float32, smallest / len(cuts), high / len(cuts))
        loudness = loudness * jnp.repeat(jnp.exp(steps), shape[dim] // blocks).reshape((-1,) + (1,) * (len(shape) - 1 - dim))
    return loudness


def bell_draw(stream_key, shape, deviation, most, shards=(), kind=jnp.bfloat16):
    values = deviation * jax.random.normal(stream_key, shape, jnp.float32)
    if shards:
        values = values * levels(stream_key, shape, shards, -0.22, 0.18)
    return jnp.clip(values, -most, most).astype(kind)


def setup_inputs(seed: int = 0, part: int = 0) -> dict:
    seeds = jax.random.split(jax.random.key(seed), 8)
    part_keys = jax.random.split(jax.random.fold_in(seeds[7], part), 8)
    conductivity = jnp.clip(jnp.exp(math.log(5.0) - 3.218876 * jax.random.uniform(part_keys[0], (NX, NY, NZ), jnp.float32) ** levels(part_keys[0], (NX, NY, NZ), ((0, 4),), -0.2, 0.2)), 0.2, 5.0)
    inverse_coefficients = draw_inverse_coefficients(jax.random.fold_in(jax.random.fold_in(seeds[7], part), 71), part)
    forward_potential = bell_draw(part_keys[2], (SOURCES, NX, NY, NZ), 1.0, 6.0, ((0, 4), (1, 4)), jnp.float32)
    misfit_field = draw_misfit_field(jax.random.fold_in(jax.random.fold_in(seeds[7], part), 71), part)
    electrodes = plant(jax.random.randint(part_keys[4], (SOURCES, 2), 0, NX * NY * NZ), jax.random.fold_in(part_keys[4], 1), 0, (NX * NY * NZ) - 1).astype(jnp.int32)
    assignment = plant(jax.random.randint(part_keys[5], (SOURCES,), 0, LINES), jax.random.fold_in(part_keys[5], 1), 0, LINES - 1).astype(jnp.int32)
    line_weight = jnp.clip(jnp.exp(jax.random.uniform(part_keys[6], (LINES,), jnp.float32, math.log(0.5), math.log(2.0))), 0.5, 2.0)
    return dict(conductivity=conductivity, inverse_coefficients=inverse_coefficients, forward_potential=forward_potential, misfit_field=misfit_field, electrodes=electrodes, assignment=assignment, line_weight=line_weight)


mass_shift = 0.05
current = 5.0
stencil_offsets = tuple((step_x - 1, step_y - 1, step_z - 1) for step_x in range(3) for step_y in range(3) for step_z in range(3))
face_offsets = ((1, 0, 0), (-1, 0, 0), (0, 1, 0), (0, -1, 0), (0, 0, 1), (0, 0, -1))


def pad_faces(field_in):
    return jnp.pad(field_in, ((0, 0), (1, 1), (1, 1), (1, 1)))


def operate_padded(padded, sigma_pad, slab_rows, height, depth_cells):
    center = padded[:, 1:1 + slab_rows, 1:1 + height, 1:1 + depth_cells]
    sigma_center = sigma_pad[1:1 + slab_rows, 1:1 + height, 1:1 + depth_cells]
    accumulated = mass_shift * center
    for step_x, step_y, step_z in face_offsets:
        beside = padded[:, 1 + step_x:1 + step_x + slab_rows, 1 + step_y:1 + step_y + height, 1 + step_z:1 + step_z + depth_cells]
        sigma_beside = sigma_pad[1 + step_x:1 + step_x + slab_rows, 1 + step_y:1 + step_y + height, 1 + step_z:1 + step_z + depth_cells]
        accumulated = accumulated + 0.5 * (sigma_center + sigma_beside) * (center - beside)
    return accumulated


def apply_forward(padded, coef_slab, slab_rows, height, depth_cells):
    accumulated = jnp.zeros((padded.shape[0], slab_rows, height, depth_cells), jnp.float32)
    for position, (step_x, step_y, step_z) in enumerate(stencil_offsets):
        accumulated = accumulated + coef_slab[position] * padded[:, 1 + step_x:1 + step_x + slab_rows, 1 + step_y:1 + step_y + height, 1 + step_z:1 + step_z + depth_cells]
    return accumulated


def apply_transposed(padded, coef_pad, slab_rows, height, depth_cells):
    accumulated = jnp.zeros((padded.shape[0], slab_rows, height, depth_cells), jnp.float32)
    for position, (step_x, step_y, step_z) in enumerate(stencil_offsets):
        coef_part = coef_pad[position, 1 - step_x:1 - step_x + slab_rows, 1 - step_y:1 - step_y + height, 1 - step_z:1 - step_z + depth_cells]
        field_part = padded[:, 1 - step_x:1 - step_x + slab_rows, 1 - step_y:1 - step_y + height, 1 - step_z:1 - step_z + depth_cells]
        accumulated = accumulated + coef_part * field_part
    return accumulated


def face_products(forward_pad, adjoint_pad, slab_rows, height, depth_cells):
    fwd_center = forward_pad[:, 1:1 + slab_rows, 1:1 + height, 1:1 + depth_cells]
    adj_center = adjoint_pad[:, 1:1 + slab_rows, 1:1 + height, 1:1 + depth_cells]
    accumulated = jnp.zeros(fwd_center.shape, jnp.float32)
    for step_x, step_y, step_z in face_offsets:
        fwd_beside = forward_pad[:, 1 + step_x:1 + step_x + slab_rows, 1 + step_y:1 + step_y + height, 1 + step_z:1 + step_z + depth_cells]
        adj_beside = adjoint_pad[:, 1 + step_x:1 + step_x + slab_rows, 1 + step_y:1 + step_y + height, 1 + step_z:1 + step_z + depth_cells]
        accumulated = accumulated + (fwd_center - fwd_beside) * (adj_center - adj_beside)
    return accumulated


def inner_sums(first_field, second_field):
    return jnp.sum(first_field * second_field, axis=(1, 2, 3))


def reference(conductivity, inverse_coefficients, forward_potential, misfit_field, electrodes, assignment, line_weight):
    sources = misfit_field.shape[0]
    total_cells = NX * NY * NZ
    source_rows = jnp.arange(sources, dtype=jnp.int32)
    charges = jnp.array([current, -current], jnp.float32)
    flattened = misfit_field.reshape(sources, total_cells).at[source_rows[:, None], electrodes].add(charges[None, :])
    right_side = flattened.reshape(misfit_field.shape)
    sigma_pad = jnp.pad(conductivity, 1)
    coef_pad = pad_faces(inverse_coefficients)

    def operate(field_in):
        return operate_padded(pad_faces(field_in), sigma_pad, NX, NY, NZ)

    def precondition(field_in):
        smooth = apply_forward(pad_faces(field_in), inverse_coefficients, NX, NY, NZ)
        return apply_transposed(pad_faces(smooth), coef_pad, NX, NY, NZ)

    adjoint = jnp.zeros_like(right_side)
    residual = right_side
    smoothed = precondition(residual)
    align_now = inner_sums(residual, smoothed)
    direction = smoothed
    for iteration in range(ITERS):
        image_field = operate(direction)
        step_size = align_now / inner_sums(direction, image_field)
        adjoint = adjoint + step_size[:, None, None, None] * direction
        residual = residual - step_size[:, None, None, None] * image_field
        if iteration + 1 < ITERS:
            smoothed = precondition(residual)
            align_next = inner_sums(residual, smoothed)
            growth = align_next / align_now
            direction = smoothed + growth[:, None, None, None] * direction
            align_now = align_next
    lines = jnp.arange(line_weight.shape[0], dtype=jnp.int32)
    weights = jnp.sum(line_weight[None, :] * (assignment[:, None] == lines[None, :]).astype(jnp.float32), axis=1)
    products = face_products(pad_faces(forward_potential), pad_faces(adjoint), NX, NY, NZ)
    gradient = -0.5 * jnp.sum(weights[:, None, None, None] * products, axis=0)
    return adjoint, gradient
```

```python
import functools

import jax
import jax.numpy as jnp
from jax import lax
from jax.experimental import pallas as pl
from jax.experimental.pallas import tpu as pltpu
from jax.sharding import PartitionSpec as P

ITERS = 2
MASS = 0.05
CURRENT = 5.0
PAD = 8
ROWS = 8
LANES = 128
CHUNKS = 9
MESH = pl.DeviceIdType.MESH


def kernel(
    dims,
    elec,
    assign,
    lines,
    sigma_hbm,
    coef_hbm,
    fwd_hbm,
    misfit_hbm,
    adj_hbm,
    grad_hbm,
    coef,
    sig,
    weights,
    res,
    dirn,
    fwd,
    adj,
    quart,
    part,
    from_left,
    from_right,
    image,
    img_left,
    img_right,
    gsum,
    grecv,
    gout,
    psend,
    precv,
    local_sem,
    out_sem,
    halo_send,
    halo_recv,
    sum_send,
    sum_recv,
    grad_send,
    grad_recv,
):
    n, nsrc, S, X, H, Z = dims
    me = lax.axis_index("space")
    mine = lax.axis_index("src")
    has_left, has_right = me > 0, me < n - 1
    left, right = lax.rem(me + n - 1, n), lax.rem(me + 1, n)
    tiles = H // ROWS
    inner = pl.ds(PAD, H)

    def plain(j):
        return pl.ds(pl.multiple_of(ROWS * j, ROWS), ROWS)

    def padded(j):
        return pl.ds(pl.multiple_of(PAD + ROWS * j, ROWS), ROWS)

    lane = lax.broadcasted_iota(jnp.int32, (ROWS, Z), 1)
    line = lax.broadcasted_iota(jnp.int32, (ROWS, Z), 0)

    def beside(ref, at, j, b):
        here = ref[(*at, padded(j), slice(None))]
        if b == 0:
            return here
        other = ref[(*at, padded(j + b), slice(None))]
        if b == 1:
            return pltpu.roll(jnp.where(line == 0, other, here), ROWS - 1, 0)
        return pltpu.roll(jnp.where(line == ROWS - 1, other, here), 1, 0)

    def along(v, c):
        if c == 0:
            return v
        if c == 1:
            return jnp.where(lane == Z - 1, 0.0, pltpu.roll(v, Z - 1, 1))
        return jnp.where(lane == 0, 0.0, pltpu.roll(v, 1, 1))

    class Halo:
        def __init__(self, slot, to_left, left_dst, to_right, right_dst):
            self.go_left = pltpu.make_async_remote_copy(
                to_left, left_dst, halo_send.at[slot, 0], halo_recv.at[slot, 0],
                device_id={"space": left}, device_id_type=MESH)
            self.go_right = pltpu.make_async_remote_copy(
                to_right, right_dst, halo_send.at[slot, 1], halo_recv.at[slot, 1],
                device_id={"space": right}, device_id_type=MESH)

        def start(self):
            pl.when(has_left)(self.go_left.start)
            pl.when(has_right)(self.go_right.start)

        def arrive(self):
            pl.when(has_right)(self.go_left.wait_recv)
            pl.when(has_left)(self.go_right.wait_recv)

        def leave(self):
            pl.when(has_left)(self.go_left.wait_send)
            pl.when(has_right)(self.go_right.wait_send)

    load_misfit = [
        pltpu.make_async_copy(misfit_hbm.at[s], res.at[s, pl.ds(1, X), inner, :], local_sem.at[s])
        for s in range(S)
    ]
    load_fwd = [
        pltpu.make_async_copy(fwd_hbm.at[s], fwd.at[s, pl.ds(1, X), inner, :], local_sem.at[S + s])
        for s in range(S)
    ]
    load_sigma = pltpu.make_async_copy(
        sigma_hbm, sig.at[pl.ds(1, X), inner, :], local_sem.at[2 * S])
    group = 27 // CHUNKS
    load_coef = [
        pltpu.make_async_copy(
            coef_hbm.at[pl.ds(group * i, group)], coef.at[pl.ds(group * i, group)],
            local_sem.at[2 * S + 1 + i])
        for i in range(CHUNKS)
    ]
    for copy in load_misfit:
        copy.start()
    for copy in load_coef:
        copy.start()
    load_sigma.start()
    for copy in load_fwd:
        copy.start()

    barrier = pltpu.get_barrier_semaphore()
    for k in range(1, n):
        pl.semaphore_signal(
            barrier, inc=1, device_id={"space": lax.rem(me + k, n)}, device_id_type=MESH)
    for k in range(1, nsrc):
        pl.semaphore_signal(
            barrier, inc=1, device_id={"src": lax.rem(mine + k, nsrc)}, device_id_type=MESH)

    for ref in (res, dirn, fwd, adj):
        edge = jnp.zeros((S, X + 2, PAD, Z), jnp.float32)
        ref[:, :, pl.ds(0, PAD), :] = edge
        ref[:, :, pl.ds(PAD + H, PAD), :] = edge
    edge = jnp.zeros((X + 2, PAD, Z), jnp.float32)
    sig[:, pl.ds(0, PAD), :] = edge
    sig[:, pl.ds(PAD + H, PAD), :] = edge
    for b in range(3):
        quart[b, :, pl.ds(0, PAD), :] = edge
        quart[b, :, pl.ds(PAD + H, PAD), :] = edge

    def clear(p):
        plane = jnp.zeros((S, H, Z), jnp.float32)
        res[:, p, inner, :] = plane
        fwd[:, p, inner, :] = plane
        sig[p, inner, :] = jnp.zeros((H, Z), jnp.float32)

    pl.when(jnp.logical_not(has_left))(lambda: clear(0))
    pl.when(jnp.logical_not(has_right))(lambda: clear(X + 1))

    pl.semaphore_wait(barrier, n - 1 + nsrc - 1)

    res_halo = [
        Halo(s, res.at[s, 1, inner, :], res.at[s, X + 1, inner, :],
             res.at[s, X, inner, :], res.at[s, 0, inner, :])
        for s in range(S)
    ]
    part_halo = [
        [
            Halo(S + it * S + s, part.at[s, pl.ds(0, 2)], from_right.at[it, s],
                 part.at[s, pl.ds(X, 2)], from_left.at[it, s])
            for s in range(S)
        ]
        for it in range(2)
    ]
    img_halo = [
        Halo(3 * S + s, image.at[s, 0], img_right.at[s], image.at[s, X - 1], img_left.at[s])
        for s in range(S)
    ]
    fwd_halo = [
        Halo(4 * S + s, fwd_hbm.at[s, 0], fwd.at[s, X + 1, inner, :],
             fwd_hbm.at[s, X - 1], fwd.at[s, 0, inner, :])
        for s in range(S)
    ]
    sig_halo = Halo(5 * S, sigma_hbm.at[0], sig.at[X + 1, inner, :],
                    sigma_hbm.at[X - 1], sig.at[0, inner, :])

    def fold(t):
        total = t[:, :LANES]
        for i in range(1, Z // LANES):
            total = total + t[:, LANES * i : LANES * (i + 1)]
        return total

    def sum_copies(slot):
        return [
            pltpu.make_async_remote_copy(
                psend.at[slot], precv.at[slot, k], sum_send.at[slot, k], sum_recv.at[slot, k],
                device_id={"space": lax.rem(me + k, n)}, device_id_type=MESH)
            for k in range(1, n)
        ]

    def sum_start(slot, t):
        psend[slot] = fold(t)
        for copy in sum_copies(slot):
            copy.start()

    def sum_finish(slot):
        total = psend[slot]
        for k, copy in enumerate(sum_copies(slot)):
            copy.wait()
            total = total + precv[slot, k + 1]
        return jnp.sum(total, keepdims=True)

    def precondition(s):
        def step(j, squares):
            sums = [jnp.zeros((ROWS, Z), jnp.float32) for _ in range(X)]
            for p in range(X + 2):
                for b in (-1, 0, 1):
                    v = beside(res, (s, p), j, b)
                    for c in (-1, 0, 1):
                        vc = along(v, c)
                        for a in (-1, 0, 1):
                            x = p - 1 - a
                            if 0 <= x < X:
                                k = 9 * (a + 1) + 3 * (b + 1) + c + 1
                                sums[x] = sums[x] + coef[k, x, plain(j), :] * vc
            for x in range(X):
                squares = squares + sums[x] * sums[x]
            for p in range(X + 2):
                for b in (-1, 0, 1):
                    total = None
                    for c in (-1, 0, 1):
                        given = None
                        for a in (-1, 0, 1):
                            x = p - 1 - a
                            if 0 <= x < X:
                                k = 9 * (a + 1) + 3 * (b + 1) + c + 1
                                term = coef[k, x, plain(j), :] * sums[x]
                                given = term if given is None else given + term
                        given = along(given, -c)
                        total = given if total is None else total + given
                    quart[b + 1, p, padded(j), :] = total
            return squares

        squares = lax.fori_loop(0, tiles, step, jnp.zeros((ROWS, Z), jnp.float32))

        def gather(j, carry):
            for p in range(X + 2):
                part[s, p, plain(j), :] = (
                    quart[1, p, padded(j), :] + beside(quart, (2, p), j, -1)
                    + beside(quart, (0, p), j, 1))
            return carry

        lax.fori_loop(0, tiles, gather, 0)
        return squares

    def find_weights():
        def step(j, carry):
            for x in range(X):
                here = sig[x + 1, padded(j), :]
                sides = (
                    sig[x + 2, padded(j), :], sig[x, padded(j), :],
                    beside(sig, (x + 1,), j, 1), beside(sig, (x + 1,), j, -1),
                    along(here, 1), along(here, -1))
                diagonal = jnp.full((ROWS, Z), MASS, jnp.float32)
                for i, side in enumerate(sides):
                    w = 0.5 * (here + side)
                    weights[i, x, plain(j), :] = w
                    diagonal = diagonal + w
                weights[6, x, plain(j), :] = diagonal
            return carry

        lax.fori_loop(0, tiles, step, 0)

    def operate(s, planes, sofar):
        def step(j, dots):
            for x in planes:
                d = dirn[s, x + 1, padded(j), :]
                sides = (
                    dirn[s, x + 2, padded(j), :], dirn[s, x, padded(j), :],
                    beside(dirn, (s, x + 1), j, 1), beside(dirn, (s, x + 1), j, -1),
                    along(d, 1), along(d, -1))
                out = weights[6, x, plain(j), :] * d
                for i, side in enumerate(sides):
                    out = out - weights[i, x, plain(j), :] * side
                image[s, x, plain(j), :] = out
                dots = dots + d * out
            return dots

        return lax.fori_loop(0, tiles, step, sofar)

    def set_direction(s, it, growth):
        def step(j, carry):
            for p in range(X + 2):
                d = part[s, p, plain(j), :]
                if p < 2:
                    d = d + jnp.where(has_left, from_left[it, s, p, plain(j), :], 0.0)
                if p >= X:
                    d = d + jnp.where(has_right, from_right[it, s, p - X, plain(j), :], 0.0)
                if p == 0:
                    d = jnp.where(has_left, d, 0.0)
                if p == X + 1:
                    d = jnp.where(has_right, d, 0.0)
                if growth is not None:
                    d = d + growth * dirn[s, p, padded(j), :]
                dirn[s, p, padded(j), :] = d
            return carry

        lax.fori_loop(0, tiles, step, 0)

    def add_step(s, size, first):
        def step(j, carry):
            for p in range(X + 2):
                v = size * dirn[s, p, padded(j), :]
                if not first:
                    v = v + adj[s, p, padded(j), :]
                adj[s, p, padded(j), :] = v
            return carry

        lax.fori_loop(0, tiles, step, 0)

    def drop_step(s, size):
        def step(j, carry):
            for x in range(X):
                res[s, x + 1, padded(j), :] = (
                    res[s, x + 1, padded(j), :] - size * image[s, x, plain(j), :])
            res[s, 0, padded(j), :] = res[s, 0, padded(j), :] - jnp.where(
                has_left, size * img_left[s, plain(j), :], 0.0)
            res[s, X + 1, padded(j), :] = res[s, X + 1, padded(j), :] - jnp.where(
                has_right, size * img_right[s, plain(j), :], 0.0)
            return carry

        lax.fori_loop(0, tiles, step, 0)

    def add_electrodes(s):
        at = lax.broadcasted_iota(jnp.int32, (ROWS, Z), 0) * Z + lane
        plus = elec[s, 0] - me * (X * H * Z)
        minus = elec[s, 1] - me * (X * H * Z)

        def step(j, carry):
            for x in range(X):
                here = at + (x * H + ROWS * j) * Z
                v = res[s, x + 1, padded(j), :]
                v = v + jnp.where(here == plus, CURRENT, 0.0)
                v = v - jnp.where(here == minus, CURRENT, 0.0)
                res[s, x + 1, padded(j), :] = v
            return carry

        lax.fori_loop(0, tiles, step, 0)

    zero = jnp.zeros((ROWS, Z), jnp.float32)
    for s in range(S):
        load_misfit[s].wait()
        add_electrodes(s)
        res_halo[s].start()
    sig_halo.start()
    for copy in load_coef:
        copy.wait()

    for s in range(S):
        res_halo[s].arrive()
        squares = precondition(s)
        part_halo[0][s].start()
        sum_start(s, squares)

    load_sigma.wait()
    sig_halo.arrive()
    find_weights()

    for s in range(S):
        part_halo[0][s].arrive()
        set_direction(s, 0, None)
        dots = operate(s, (0, X - 1), zero)
        img_halo[s].start()
        dots = operate(s, tuple(range(1, X - 1)), dots)
        sum_start(S + s, dots)
    for s in range(S):
        fwd_halo[s].start()

    align = []
    for s in range(S):
        align.append(sum_finish(s))
        size = align[s] / sum_finish(S + s)
        add_step(s, size, True)
        img_halo[s].arrive()
        res_halo[s].leave()
        drop_step(s, size)
        part_halo[0][s].leave()
        squares = precondition(s)
        part_halo[1][s].start()
        sum_start(2 * S + s, squares)

    for s in range(S):
        part_halo[1][s].arrive()
        now = sum_finish(2 * S + s)
        set_direction(s, 1, now / align[s])
        align[s] = now
        img_halo[s].leave()
        dots = operate(s, tuple(range(X)), zero)
        sum_start(3 * S + s, dots)

    save = []
    for s in range(S):
        size = align[s] / sum_finish(3 * S + s)
        add_step(s, size, False)
        save.append(pltpu.make_async_copy(
            adj.at[s, pl.ds(1, X), inner, :], adj_hbm.at[s], out_sem.at[s]))
        save[s].start()
    for s in range(S):
        load_fwd[s].wait()
        fwd_halo[s].arrive()

    scale = []
    for s in range(S):
        w = jnp.float32(0.0)
        for i in range(lines.shape[0]):
            w = w + jnp.where(assign[s] == i, lines[i], 0.0)
        scale.append(-0.5 * w)

    def gradient(j, carry):
        for x in range(X):
            total = None
            for s in range(S):
                f, a = fwd[s, x + 1, padded(j), :], adj[s, x + 1, padded(j), :]
                sides = [
                    (r[s, x + 2, padded(j), :], r[s, x, padded(j), :],
                     beside(r, (s, x + 1), j, 1), beside(r, (s, x + 1), j, -1),
                     along(v, 1), along(v, -1))
                    for r, v in ((fwd, f), (adj, a))
                ]
                sums = None
                for fs, as_ in zip(*sides):
                    term = (f - fs) * (a - as_)
                    sums = term if sums is None else sums + term
                term = scale[s] * sums
                total = term if total is None else total + term
            gsum[x, plain(j), :] = total
        return carry

    lax.fori_loop(0, tiles, gradient, 0)

    count = H // nsrc

    def share(t):
        return pl.ds(pl.multiple_of(count * t, count), count)

    give = []
    for k in range(1, nsrc):
        to = lax.rem(mine + k, nsrc)
        give.append(pltpu.make_async_remote_copy(
            gsum.at[:, share(to), :], grecv.at[k - 1], grad_send.at[k], grad_recv.at[k],
            device_id={"src": to}, device_id_type=MESH))
        give[-1].start()
    total = gsum[:, share(mine), :]
    for k in range(1, nsrc):
        give[k - 1].wait()
        total = total + grecv[k - 1]
    gout[...] = total
    last = pltpu.make_async_copy(gout, grad_hbm, out_sem.at[S])
    last.start()

    for s in range(S):
        part_halo[1][s].leave()
        fwd_halo[s].leave()
        save[s].wait()
    sig_halo.leave()
    last.wait()


def body(n, nsrc, conductivity, inverse_coefficients, forward_potential, misfit_field,
         electrodes, assignment, line_weight):
    S, X, H, Z = misfit_field.shape
    f32 = jnp.float32
    tall = H + 2 * PAD
    field = pltpu.VMEM((S, X + 2, tall, Z), f32)
    dma = pltpu.SemaphoreType.DMA
    smem = pl.BlockSpec(memory_space=pltpu.SMEM)
    anywhere = pl.BlockSpec(memory_space=pl.ANY)
    return pl.pallas_call(
        functools.partial(kernel, (n, nsrc, S, X, H, Z)),
        out_shape=(
            jax.ShapeDtypeStruct((S, X, H, Z), f32),
            jax.ShapeDtypeStruct((X, H // nsrc, Z), f32),
        ),
        in_specs=[smem] * 3 + [anywhere] * 4,
        out_specs=(anywhere, anywhere),
        scratch_shapes=[
            pltpu.VMEM((27, X, H, Z), f32),
            pltpu.VMEM((X + 2, tall, Z), f32),
            pltpu.VMEM((7, X, H, Z), f32),
            field, field, field, field,
            pltpu.VMEM((3, X + 2, tall, Z), f32),
            pltpu.VMEM((S, X + 2, H, Z), f32),
            pltpu.VMEM((ITERS, S, 2, H, Z), f32),
            pltpu.VMEM((ITERS, S, 2, H, Z), f32),
            pltpu.VMEM((S, X, H, Z), f32),
            pltpu.VMEM((S, H, Z), f32),
            pltpu.VMEM((S, H, Z), f32),
            pltpu.VMEM((X, H, Z), f32),
            pltpu.VMEM((nsrc - 1, X, H // nsrc, Z), f32),
            pltpu.VMEM((X, H // nsrc, Z), f32),
            pltpu.VMEM((4 * S, ROWS, LANES), f32),
            pltpu.VMEM((4 * S, n, ROWS, LANES), f32),
            dma((2 * S + 1 + CHUNKS,)),
            dma((S + 1,)),
            dma((5 * S + 1, 2)),
            dma((5 * S + 1, 2)),
            dma((4 * S, n)),
            dma((4 * S, n)),
            dma((nsrc,)),
            dma((nsrc,)),
        ],
        compiler_params=pltpu.CompilerParams(
            collective_id=0, has_side_effects=True, vmem_limit_bytes=60 * 1024 * 1024),
    )(electrodes, assignment, line_weight, conductivity, inverse_coefficients,
      forward_potential, misfit_field)


def solution(mesh):
    in_specs = (
        P(("groups", "space"), None, None),
        P(None, ("groups", "space"), None, None),
        P(("groups", "src"), "space", None, None),
        P(("groups", "src"), "space", None, None),
        P(("groups", "src"), None),
        P(("groups", "src")),
        P("groups"),
    )
    out_specs = (P(("groups", "src"), "space", None, None), P(("groups", "space"), "src", None))
    run = functools.partial(body, mesh.shape["space"], mesh.shape["src"])
    return jax.shard_map(run, mesh=mesh, in_specs=in_specs, out_specs=out_specs, check_vma=False)
```

```python
import functools

import jax
import jax.numpy as jnp
from jax import lax
from jax.experimental import pallas as pl
from jax.experimental.pallas import tpu as pltpu
from jax.sharding import PartitionSpec as P

ITERS = 2
MASS = 0.05
CURRENT = 5.0
PAD = 8
ROWS = 8
LANES = 128
CHUNKS = 9
MESH = pl.DeviceIdType.MESH


def kernel(
    dims,
    elec,
    assign,
    lines,
    sigma_hbm,
    coef_hbm,
    fwd_hbm,
    misfit_hbm,
    adj_hbm,
    grad_hbm,
    coef,
    sig,
    weights,
    res,
    fwd,
    img,
    next_dir,
    first_dir,
    smooth,
    quart,
    part,
    from_left,
    from_right,
    gsum,
    gpart,
    out,
    grecv,
    gout,
    psend,
    precv,
    local_sem,
    out_sem,
    halo_send,
    halo_recv,
    sum_send,
    sum_recv,
    grad_send,
    grad_recv,
):
    n, nsrc, S, X, H, Z = dims
    me = lax.axis_index("space")
    mine = lax.axis_index("src")
    has_left, has_right = me > 0, me < n - 1
    left, right = lax.rem(me + n - 1, n), lax.rem(me + 1, n)
    tiles = H // ROWS
    inner = pl.ds(PAD, H)

    def plain(j):
        return pl.ds(pl.multiple_of(ROWS * j, ROWS), ROWS)

    def padded(j):
        return pl.ds(pl.multiple_of(PAD + ROWS * j, ROWS), ROWS)

    lane = lax.broadcasted_iota(jnp.int32, (ROWS, Z), 1)
    zero = jnp.zeros((ROWS, Z), jnp.float32)
    line = lax.broadcasted_iota(jnp.int32, (ROWS, Z), 0)

    def beside(ref, at, j, b):
        here = ref[(*at, padded(j), slice(None))]
        if b == 0:
            return here
        other = ref[(*at, padded(j + b), slice(None))]
        if b == 1:
            return pltpu.roll(jnp.where(line == 0, other, here), ROWS - 1, 0)
        return pltpu.roll(jnp.where(line == ROWS - 1, other, here), 1, 0)

    def along(v, c):
        if c == 0:
            return v
        if c == 1:
            return jnp.where(lane == Z - 1, 0.0, pltpu.roll(v, Z - 1, 1))
        return jnp.where(lane == 0, 0.0, pltpu.roll(v, 1, 1))

    class Halo:
        def __init__(self, slot, to_left, left_dst, to_right, right_dst):
            self.go_left = pltpu.make_async_remote_copy(
                to_left, left_dst, halo_send.at[slot, 0], halo_recv.at[slot, 0],
                device_id={"space": left}, device_id_type=MESH)
            self.go_right = pltpu.make_async_remote_copy(
                to_right, right_dst, halo_send.at[slot, 1], halo_recv.at[slot, 1],
                device_id={"space": right}, device_id_type=MESH)

        def start(self):
            pl.when(has_left)(self.go_left.start)
            pl.when(has_right)(self.go_right.start)

        def arrive(self):
            pl.when(has_right)(self.go_left.wait_recv)
            pl.when(has_left)(self.go_right.wait_recv)

        def leave(self):
            pl.when(has_left)(self.go_left.wait_send)
            pl.when(has_right)(self.go_right.wait_send)

    load_misfit = [
        pltpu.make_async_copy(misfit_hbm.at[s], res.at[s, pl.ds(1, X), inner, :], local_sem.at[s])
        for s in range(S)
    ]
    load_fwd = [
        pltpu.make_async_copy(fwd_hbm.at[s], fwd.at[s, pl.ds(1, X), inner, :], local_sem.at[S + s])
        for s in range(S)
    ]
    load_sigma = pltpu.make_async_copy(
        sigma_hbm, sig.at[pl.ds(2, X), inner, :], local_sem.at[2 * S])
    group = 27 // CHUNKS
    load_coef = [
        pltpu.make_async_copy(
            coef_hbm.at[pl.ds(group * i, group)], coef.at[pl.ds(group * i, group)],
            local_sem.at[2 * S + 1 + i])
        for i in range(CHUNKS)
    ]
    for copy in load_misfit:
        copy.start()
    for copy in load_coef:
        copy.start()
    load_sigma.start()
    for copy in load_fwd:
        copy.start()

    barrier = pltpu.get_barrier_semaphore()
    for k in range(1, n):
        pl.semaphore_signal(
            barrier, inc=1, device_id={"space": lax.rem(me + k, n)}, device_id_type=MESH)
    for k in range(1, nsrc):
        pl.semaphore_signal(
            barrier, inc=1, device_id={"src": lax.rem(mine + k, nsrc)}, device_id_type=MESH)

    def clear_rows(ref):
        planes = ref.shape[0]
        edge = jnp.zeros((planes, PAD, Z), jnp.float32)
        ref[:, pl.ds(0, PAD), :] = edge
        ref[:, pl.ds(PAD + H, PAD), :] = edge

    for s in range(S):
        for ref in (res, fwd, img, next_dir, first_dir):
            clear_rows(ref.at[s])
    clear_rows(sig)
    for b in range(3):
        clear_rows(quart.at[b])

    def clear(p, q):
        plane = jnp.zeros((S, H, Z), jnp.float32)
        res[:, p, inner, :] = plane
        fwd[:, p, inner, :] = plane
        sig[pl.ds(q, 2), inner, :] = jnp.zeros((2, H, Z), jnp.float32)

    pl.when(jnp.logical_not(has_left))(lambda: clear(0, 0))
    pl.when(jnp.logical_not(has_right))(lambda: clear(X + 1, X + 2))

    pl.semaphore_wait(barrier, n - 1 + nsrc - 1)

    res_halo = [
        Halo(s, res.at[s, 1, inner, :], res.at[s, X + 1, inner, :],
             res.at[s, X, inner, :], res.at[s, 0, inner, :])
        for s in range(S)
    ]
    part_halo = [
        [
            Halo(S + s, part.at[0, s, pl.ds(0, 3)], from_right.at[0, s],
                 part.at[0, s, pl.ds(X - 1, 3)], from_left.at[0, s])
            for s in range(S)
        ],
        [
            Halo(2 * S + s, part.at[1, s, pl.ds(0, 2)], from_right.at[1, s, pl.ds(0, 2)],
                 part.at[1, s, pl.ds(X, 2)], from_left.at[1, s, pl.ds(1, 2)])
            for s in range(S)
        ],
    ]
    fwd_halo = [
        Halo(3 * S + s, fwd_hbm.at[s, 0], fwd.at[s, X + 1, inner, :],
             fwd_hbm.at[s, X - 1], fwd.at[s, 0, inner, :])
        for s in range(S)
    ]
    sig_halo = Halo(4 * S, sigma_hbm.at[pl.ds(0, 2)], sig.at[pl.ds(X + 2, 2), inner, :],
                    sigma_hbm.at[pl.ds(X - 2, 2)], sig.at[pl.ds(0, 2), inner, :])

    def fold(t):
        total = t[:, :LANES]
        for i in range(1, Z // LANES):
            total = total + t[:, LANES * i : LANES * (i + 1)]
        return total

    def sum_copies(slot, count):
        some = pl.ds(0, count)
        return [
            pltpu.make_async_remote_copy(
                psend.at[slot, some], precv.at[slot, k, some],
                sum_send.at[slot, k], sum_recv.at[slot, k],
                device_id={"space": lax.rem(me + k, n)}, device_id_type=MESH)
            for k in range(1, n)
        ]

    def sum_start(slot, *terms):
        for i, t in enumerate(terms):
            psend[slot, i] = fold(t)
        for copy in sum_copies(slot, len(terms)):
            copy.start()

    def sum_finish(slot, count=1):
        totals = [psend[slot, i] for i in range(count)]
        for k, copy in enumerate(sum_copies(slot, count)):
            copy.wait()
            totals = [t + precv[slot, k + 1, i] for i, t in enumerate(totals)]
        totals = [jnp.sum(t, keepdims=True) for t in totals]
        return totals if count > 1 else totals[0]

    def precondition(field, it, s):
        def step(j, carry):
            squares, cross = carry
            sums = [jnp.zeros((ROWS, Z), jnp.float32) for _ in range(X)]
            for p in range(X + 2):
                for b in (-1, 0, 1):
                    v = beside(field, (s, p), j, b)
                    for c in (-1, 0, 1):
                        vc = along(v, c)
                        for a in (-1, 0, 1):
                            x = p - 1 - a
                            if 0 <= x < X:
                                k = 9 * (a + 1) + 3 * (b + 1) + c + 1
                                sums[x] = sums[x] + coef[k, x, plain(j), :] * vc
            for x in range(X):
                if it == 0:
                    smooth[s, x, plain(j), :] = sums[x]
                else:
                    cross = cross + sums[x] * smooth[s, x, plain(j), :]
                squares = squares + sums[x] * sums[x]
            for p in range(X + 2):
                for b in (-1, 0, 1):
                    total = None
                    for c in (-1, 0, 1):
                        given = None
                        for a in (-1, 0, 1):
                            x = p - 1 - a
                            if 0 <= x < X:
                                k = 9 * (a + 1) + 3 * (b + 1) + c + 1
                                term = coef[k, x, plain(j), :] * sums[x]
                                given = term if given is None else given + term
                        given = along(given, -c)
                        total = given if total is None else total + given
                    quart[b + 1, p, padded(j), :] = total
            return squares, cross

        squares, cross = lax.fori_loop(0, tiles, step, (zero, zero))

        def gather(j, carry):
            for p in range(X + 2):
                part[it, s, p, plain(j), :] = (
                    quart[1, p, padded(j), :] + beside(quart, (2, p), j, -1)
                    + beside(quart, (0, p), j, 1))
            return carry

        lax.fori_loop(0, tiles, gather, 0)
        return squares, cross

    def find_weights():
        def step(j, carry):
            for x in range(-1, X + 1):
                here = sig[x + 2, padded(j), :]
                sides = (
                    sig[x + 3, padded(j), :], sig[x + 1, padded(j), :],
                    beside(sig, (x + 2,), j, 1), beside(sig, (x + 2,), j, -1),
                    along(here, 1), along(here, -1))
                diagonal = jnp.full((ROWS, Z), MASS, jnp.float32)
                for i, side in enumerate(sides):
                    w = 0.5 * (here + side)
                    weights[i, x + 1, plain(j), :] = w
                    diagonal = diagonal + w
                weights[6, x + 1, plain(j), :] = diagonal
            return carry

        lax.fori_loop(0, tiles, step, 0)

    def operate(field, s, low, high, keep):
        def step(j, dots):
            for x in range(low, high):
                d = field[s, x + 2, padded(j), :]
                sides = (
                    field[s, x + 3, padded(j), :], field[s, x + 1, padded(j), :],
                    beside(field, (s, x + 2), j, 1), beside(field, (s, x + 2), j, -1),
                    along(d, 1), along(d, -1))
                total = weights[6, x + 1, plain(j), :] * d
                for i, side in enumerate(sides):
                    total = total - weights[i, x + 1, plain(j), :] * side
                if 0 <= x < X:
                    dots = dots + d * total
                if x < 0:
                    total = jnp.where(has_left, total, 0.0)
                if x >= X:
                    total = jnp.where(has_right, total, 0.0)
                if keep:
                    img[s, x + 1, padded(j), :] = total
            return dots

        return lax.fori_loop(0, tiles, step, zero)

    def complete(it, s, x, j):
        total = part[it, s, x + 1, plain(j), :] if -1 <= x <= X else None
        if x < 1:
            there = from_left[it, s, x + 2, plain(j), :]
            if total is not None:
                there = total + there
            total = jnp.where(has_left, there, 0.0 if x < 0 else total)
        if x > X - 2:
            there = from_right[it, s, x - X + 1, plain(j), :]
            if total is not None:
                there = total + there
            total = jnp.where(has_right, there, 0.0 if x >= X else total)
        return total

    def set_first(s):
        def step(j, carry):
            for x in range(-2, X + 2):
                first_dir[s, x + 2, padded(j), :] = complete(0, s, x, j)
            return carry

        lax.fori_loop(0, tiles, step, 0)

    def set_next(s, size, growth):
        def step(j, carry):
            for x in range(-1, X + 1):
                d = first_dir[s, x + 2, padded(j), :]
                next_dir[s, x + 2, padded(j), :] = (
                    (d - size * complete(1, s, x, j)) + growth * d)
            return carry

        lax.fori_loop(0, tiles, step, 0)

    def face_terms(field, s, factor, into, add):
        def step(j, carry):
            for x in range(X):
                f, a = fwd[s, x + 1, padded(j), :], field[s, x + 2, padded(j), :]
                sides = [
                    (r[s, x + at + 1, padded(j), :], r[s, x + at - 1, padded(j), :],
                     beside(r, (s, x + at), j, 1), beside(r, (s, x + at), j, -1),
                     along(v, 1), along(v, -1))
                    for r, v, at in ((fwd, f, 1), (field, a, 2))
                ]
                sums = None
                for fs, as_ in zip(*sides):
                    term = (f - fs) * (a - as_)
                    sums = term if sums is None else sums + term
                term = factor * sums
                if add:
                    term = term + into[x, plain(j), :]
                into[x, plain(j), :] = term
            return carry

        lax.fori_loop(0, tiles, step, 0)

    def add_electrodes(s):
        at = lax.broadcasted_iota(jnp.int32, (ROWS, Z), 0) * Z + lane
        plus = elec[s, 0] - me * (X * H * Z)
        minus = elec[s, 1] - me * (X * H * Z)

        def step(j, carry):
            for x in range(X):
                here = at + (x * H + ROWS * j) * Z
                v = res[s, x + 1, padded(j), :]
                v = v + jnp.where(here == plus, CURRENT, 0.0)
                v = v - jnp.where(here == minus, CURRENT, 0.0)
                res[s, x + 1, padded(j), :] = v
            return carry

        lax.fori_loop(0, tiles, step, 0)

    scale = []
    for s in range(S):
        w = jnp.float32(0.0)
        for i in range(lines.shape[0]):
            w = w + jnp.where(assign[s] == i, lines[i], 0.0)
        scale.append(-0.5 * w)

    for s in range(S):
        load_misfit[s].wait()
        add_electrodes(s)
        res_halo[s].start()
    sig_halo.start()
    fwd_halo[0].start()
    for copy in load_coef:
        copy.wait()

    for s in range(S):
        res_halo[s].arrive()
        squares, _ = precondition(res, 0, s)
        sum_start(s, squares)
        part_halo[0][s].start()
        if s == 0:
            load_sigma.wait()
            sig_halo.arrive()
            find_weights()

    fwd_halo[1].start()
    align, size = [], []
    for s in range(S):
        part_halo[0][s].arrive()
        set_first(s)
        sum_start(S + s, operate(first_dir, s, -1, X + 1, True))
        sum_start(2 * S + s, *precondition(img, 1, s))
        part_halo[1][s].start()

    for s in range(S):
        align.append(sum_finish(s))
        size.append(align[s] / sum_finish(S + s))
    for s in range(S):
        load_fwd[s].wait()
        fwd_halo[s].arrive()
        face_terms(first_dir, s, scale[s] * size[s], gsum, s > 0)

    for s in range(S):
        part_halo[1][s].arrive()
        squares, cross = sum_finish(2 * S + s, 2)
        now = align[s] - size[s] * (2.0 * cross - size[s] * squares)
        set_next(s, size[s], now / align[s])
        align[s] = now
        sum_start(3 * S + s, operate(next_dir, s, 0, X, False))
    for s in range(S):
        face_terms(next_dir, s, scale[s], gpart.at[s], False)

    last_size = [align[s] / sum_finish(3 * S + s) for s in range(S)]

    def combine(j, carry):
        for x in range(X):
            total = gsum[x, plain(j), :]
            for s in range(S):
                total = total + last_size[s] * gpart[s, x, plain(j), :]
            gsum[x, plain(j), :] = total
        return carry

    lax.fori_loop(0, tiles, combine, 0)

    count = H // nsrc

    def share(t):
        return pl.ds(pl.multiple_of(count * t, count), count)

    give = []
    for k in range(1, nsrc):
        to = lax.rem(mine + k, nsrc)
        give.append(pltpu.make_async_remote_copy(
            gsum.at[:, share(to), :], grecv.at[k - 1], grad_send.at[k], grad_recv.at[k],
            device_id={"src": to}, device_id_type=MESH))
        give[-1].start()

    save = []
    for s in range(S):

        def add_up(j, carry, s=s):
            for x in range(X):
                out[s, x, plain(j), :] = (
                    size[s] * first_dir[s, x + 2, padded(j), :]
                    + last_size[s] * next_dir[s, x + 2, padded(j), :])
            return carry

        lax.fori_loop(0, tiles, add_up, 0)
        save.append(pltpu.make_async_copy(out.at[s], adj_hbm.at[s], out_sem.at[s]))
        save[s].start()

    total = gsum[:, share(mine), :]
    for k in range(1, nsrc):
        give[k - 1].wait()
        total = total + grecv[k - 1]
    gout[...] = total
    last = pltpu.make_async_copy(gout, grad_hbm, out_sem.at[S])
    last.start()

    for s in range(S):
        res_halo[s].leave()
        part_halo[0][s].leave()
        part_halo[1][s].leave()
        fwd_halo[s].leave()
        save[s].wait()
    sig_halo.leave()
    last.wait()


def body(n, nsrc, conductivity, inverse_coefficients, forward_potential, misfit_field,
         electrodes, assignment, line_weight):
    S, X, H, Z = misfit_field.shape
    f32 = jnp.float32
    tall = H + 2 * PAD
    field = pltpu.VMEM((S, X + 2, tall, Z), f32)
    wide = pltpu.VMEM((S, X + 4, tall, Z), f32)
    dma = pltpu.SemaphoreType.DMA
    smem = pl.BlockSpec(memory_space=pltpu.SMEM)
    anywhere = pl.BlockSpec(memory_space=pl.ANY)
    shapes = (
        jax.ShapeDtypeStruct((S, X, H, Z), f32),
        jax.ShapeDtypeStruct((X, H // nsrc, Z), f32),
    )
    results = pl.pallas_call(
        functools.partial(kernel, (n, nsrc, S, X, H, Z)),
        out_shape=shapes,
        in_specs=[smem] * 3 + [anywhere] * 4,
        out_specs=(anywhere, anywhere),
        scratch_shapes=[
            pltpu.VMEM((27, X, H, Z), f32),
            pltpu.VMEM((X + 4, tall, Z), f32),
            pltpu.VMEM((7, X + 2, H, Z), f32),
            field, field, field, wide, wide,
            pltpu.VMEM((S, X, H, Z), f32),
            pltpu.VMEM((3, X + 2, tall, Z), f32),
            pltpu.VMEM((ITERS, S, X + 2, H, Z), f32),
            pltpu.VMEM((ITERS, S, 3, H, Z), f32),
            pltpu.VMEM((ITERS, S, 3, H, Z), f32),
            pltpu.VMEM((X, H, Z), f32),
            pltpu.VMEM((S, X, H, Z), f32),
            pltpu.VMEM((S, X, H, Z), f32),
            pltpu.VMEM((nsrc - 1, X, H // nsrc, Z), f32),
            pltpu.VMEM((X, H // nsrc, Z), f32),
            pltpu.VMEM((4 * S, 2, ROWS, LANES), f32),
            pltpu.VMEM((4 * S, n, 2, ROWS, LANES), f32),
            dma((2 * S + 1 + CHUNKS,)),
            dma((S + 1,)),
            dma((4 * S + 1, 2)),
            dma((4 * S + 1, 2)),
            dma((4 * S, n)),
            dma((4 * S, n)),
            dma((nsrc,)),
            dma((nsrc,)),
        ],
        compiler_params=pltpu.CompilerParams(
            collective_id=0, has_side_effects=True, vmem_limit_bytes=60 * 1024 * 1024),
    )(electrodes, assignment, line_weight, conductivity, inverse_coefficients,
      forward_potential, misfit_field)
    return pl.pallas_call(
        hand_over,
        out_shape=shapes,
        in_specs=[pl.BlockSpec(memory_space=pltpu.VMEM)] * 2,
        out_specs=(pl.BlockSpec(memory_space=pltpu.VMEM),) * 2,
    )(*results)


def hand_over(adj, grad, adj_out, grad_out):
    adj_out[...] = adj[...]
    grad_out[...] = grad[...]


def solution(mesh):
    in_specs = (
        P(("groups", "space"), None, None),
        P(None, ("groups", "space"), None, None),
        P(("groups", "src"), "space", None, None),
        P(("groups", "src"), "space", None, None),
        P(("groups", "src"), None),
        P(("groups", "src")),
        P("groups"),
    )
    out_specs = (P(("groups", "src"), "space", None, None), P(("groups", "space"), "src", None))
    run = functools.partial(body, mesh.shape["space"], mesh.shape["src"])
    return jax.shard_map(run, mesh=mesh, in_specs=in_specs, out_specs=out_specs, check_vma=False)
```

```python
import functools

import jax
import jax.numpy as jnp
from jax import lax
from jax.experimental import pallas as pl
from jax.experimental.pallas import tpu as pltpu
from jax.sharding import PartitionSpec as P

ITERS = 2
MASS = 0.05
CURRENT = 5.0
PAD = 8
ROWS = 8
LANES = 128
CHUNKS = 9
MESH = pl.DeviceIdType.MESH


def kernel(
    dims,
    elec,
    assign,
    lines,
    sigma_hbm,
    coef_hbm,
    fwd_hbm,
    misfit_hbm,
    adj_hbm,
    grad_hbm,
    coef,
    sig,
    weights,
    res,
    fwd,
    img,
    next_dir,
    first_dir,
    smooth,
    quart,
    part,
    from_left,
    from_right,
    gsum,
    gpart,
    out,
    grecv,
    gout,
    psend,
    precv,
    local_sem,
    out_sem,
    halo_send,
    halo_recv,
    sum_send,
    sum_recv,
    grad_send,
    grad_recv,
):
    n, nsrc, S, X, H, Z = dims
    me = lax.axis_index("space")
    mine = lax.axis_index("src")
    has_left, has_right = me > 0, me < n - 1
    left, right = lax.rem(me + n - 1, n), lax.rem(me + 1, n)
    tiles = H // ROWS
    inner = pl.ds(PAD, H)

    def plain(j):
        return pl.ds(pl.multiple_of(ROWS * j, ROWS), ROWS)

    def padded(j):
        return pl.ds(pl.multiple_of(PAD + ROWS * j, ROWS), ROWS)

    lane = lax.broadcasted_iota(jnp.int32, (ROWS, Z), 1)
    zero = jnp.zeros((ROWS, Z), jnp.float32)
    line = lax.broadcasted_iota(jnp.int32, (ROWS, Z), 0)

    def beside(ref, at, j, b):
        here = ref[(*at, padded(j), slice(None))]
        if b == 0:
            return here
        other = ref[(*at, padded(j + b), slice(None))]
        if b == 1:
            return pltpu.roll(jnp.where(line == 0, other, here), ROWS - 1, 0)
        return pltpu.roll(jnp.where(line == ROWS - 1, other, here), 1, 0)

    def along(v, c):
        if c == 0:
            return v
        if c == 1:
            return jnp.where(lane == Z - 1, 0.0, pltpu.roll(v, Z - 1, 1))
        return jnp.where(lane == 0, 0.0, pltpu.roll(v, 1, 1))

    class Halo:
        def __init__(self, slot, to_left, left_dst, to_right, right_dst):
            self.go_left = pltpu.make_async_remote_copy(
                to_left, left_dst, halo_send.at[slot, 0], halo_recv.at[slot, 0],
                device_id={"space": left}, device_id_type=MESH)
            self.go_right = pltpu.make_async_remote_copy(
                to_right, right_dst, halo_send.at[slot, 1], halo_recv.at[slot, 1],
                device_id={"space": right}, device_id_type=MESH)

        def start(self):
            pl.when(has_left)(self.go_left.start)
            pl.when(has_right)(self.go_right.start)

        def arrive(self):
            pl.when(has_right)(self.go_left.wait_recv)
            pl.when(has_left)(self.go_right.wait_recv)

        def leave(self):
            pl.when(has_left)(self.go_left.wait_send)
            pl.when(has_right)(self.go_right.wait_send)

    load_misfit = [
        pltpu.make_async_copy(misfit_hbm.at[s], res.at[s, pl.ds(1, X), inner, :], local_sem.at[s])
        for s in range(S)
    ]
    load_fwd = [
        pltpu.make_async_copy(fwd_hbm.at[s], fwd.at[s, pl.ds(1, X), inner, :], local_sem.at[S + s])
        for s in range(S)
    ]
    load_sigma = pltpu.make_async_copy(
        sigma_hbm, sig.at[pl.ds(2, X), inner, :], local_sem.at[2 * S])
    group = 27 // CHUNKS
    load_coef = [
        pltpu.make_async_copy(
            coef_hbm.at[pl.ds(group * i, group)], coef.at[pl.ds(group * i, group)],
            local_sem.at[2 * S + 1 + i])
        for i in range(CHUNKS)
    ]
    for copy in load_misfit:
        copy.start()
    for copy in load_coef:
        copy.start()
    load_sigma.start()
    for copy in load_fwd:
        copy.start()

    barrier = pltpu.get_barrier_semaphore()
    for k in range(1, n):
        pl.semaphore_signal(
            barrier, inc=1, device_id={"space": lax.rem(me + k, n)}, device_id_type=MESH)
    for k in range(1, nsrc):
        pl.semaphore_signal(
            barrier, inc=1, device_id={"src": lax.rem(mine + k, nsrc)}, device_id_type=MESH)

    def clear_rows(ref):
        planes = ref.shape[0]
        edge = jnp.zeros((planes, PAD, Z), jnp.float32)
        ref[:, pl.ds(0, PAD), :] = edge
        ref[:, pl.ds(PAD + H, PAD), :] = edge

    for s in range(S):
        for ref in (res, fwd, img, next_dir, first_dir):
            clear_rows(ref.at[s])
    clear_rows(sig)
    for b in range(3):
        clear_rows(quart.at[b])

    def clear(p, q):
        plane = jnp.zeros((S, H, Z), jnp.float32)
        res[:, p, inner, :] = plane
        fwd[:, p, inner, :] = plane
        sig[pl.ds(q, 2), inner, :] = jnp.zeros((2, H, Z), jnp.float32)

    pl.when(jnp.logical_not(has_left))(lambda: clear(0, 0))
    pl.when(jnp.logical_not(has_right))(lambda: clear(X + 1, X + 2))

    pl.semaphore_wait(barrier, n - 1 + nsrc - 1)

    res_halo = [
        Halo(s, res.at[s, 1, inner, :], res.at[s, X + 1, inner, :],
             res.at[s, X, inner, :], res.at[s, 0, inner, :])
        for s in range(S)
    ]
    part_halo = [
        [
            Halo(S + s, part.at[0, s, pl.ds(0, 3)], from_right.at[0, s],
                 part.at[0, s, pl.ds(X - 1, 3)], from_left.at[0, s])
            for s in range(S)
        ],
        [
            Halo(2 * S + s, part.at[1, s, pl.ds(0, 2)], from_right.at[1, s, pl.ds(0, 2)],
                 part.at[1, s, pl.ds(X, 2)], from_left.at[1, s, pl.ds(1, 2)])
            for s in range(S)
        ],
    ]
    fwd_halo = [
        Halo(3 * S + s, fwd_hbm.at[s, 0], fwd.at[s, X + 1, inner, :],
             fwd_hbm.at[s, X - 1], fwd.at[s, 0, inner, :])
        for s in range(S)
    ]
    sig_halo = Halo(4 * S, sigma_hbm.at[pl.ds(0, 2)], sig.at[pl.ds(X + 2, 2), inner, :],
                    sigma_hbm.at[pl.ds(X - 2, 2)], sig.at[pl.ds(0, 2), inner, :])

    def fold(t):
        total = t[:, :LANES]
        for i in range(1, Z // LANES):
            total = total + t[:, LANES * i : LANES * (i + 1)]
        return total

    def sum_copies(slot, count):
        some = pl.ds(0, count)
        return [
            pltpu.make_async_remote_copy(
                psend.at[slot, some], precv.at[slot, k, some],
                sum_send.at[slot, k], sum_recv.at[slot, k],
                device_id={"space": lax.rem(me + k, n)}, device_id_type=MESH)
            for k in range(1, n)
        ]

    def sum_start(slot, *terms):
        for i, t in enumerate(terms):
            psend[slot, i] = fold(t)
        for copy in sum_copies(slot, len(terms)):
            copy.start()

    def sum_finish(slot, count=1):
        totals = [psend[slot, i] for i in range(count)]
        for k, copy in enumerate(sum_copies(slot, count)):
            copy.wait()
            totals = [t + precv[slot, k + 1, i] for i, t in enumerate(totals)]
        totals = [jnp.sum(t, keepdims=True) for t in totals]
        return totals if count > 1 else totals[0]

    def precondition(field, it, s):
        def step(j, carry):
            squares, cross = carry
            sums = [jnp.zeros((ROWS, Z), jnp.float32) for _ in range(X)]
            for p in range(X + 2):
                for b in (-1, 0, 1):
                    v = beside(field, (s, p), j, b)
                    for c in (-1, 0, 1):
                        vc = along(v, c)
                        for a in (-1, 0, 1):
                            x = p - 1 - a
                            if 0 <= x < X:
                                k = 9 * (a + 1) + 3 * (b + 1) + c + 1
                                sums[x] = sums[x] + coef[k, x, plain(j), :] * vc
            for x in range(X):
                if it == 0:
                    smooth[s, x, plain(j), :] = sums[x]
                else:
                    cross = cross + sums[x] * smooth[s, x, plain(j), :]
                squares = squares + sums[x] * sums[x]
            for p in range(X + 2):
                for b in (-1, 0, 1):
                    total = None
                    for c in (-1, 0, 1):
                        given = None
                        for a in (-1, 0, 1):
                            x = p - 1 - a
                            if 0 <= x < X:
                                k = 9 * (a + 1) + 3 * (b + 1) + c + 1
                                term = coef[k, x, plain(j), :] * sums[x]
                                given = term if given is None else given + term
                        given = along(given, -c)
                        total = given if total is None else total + given
                    quart[b + 1, p, padded(j), :] = total
            return squares, cross

        squares, cross = lax.fori_loop(0, tiles, step, (zero, zero))

        def gather(j, carry):
            for p in range(X + 2):
                part[it, s, p, plain(j), :] = (
                    quart[1, p, padded(j), :] + beside(quart, (2, p), j, -1)
                    + beside(quart, (0, p), j, 1))
            return carry

        lax.fori_loop(0, tiles, gather, 0, unroll=4)
        return squares, cross

    def find_weights():
        def step(j, carry):
            for x in range(-1, X + 1):
                here = sig[x + 2, padded(j), :]
                sides = (
                    sig[x + 3, padded(j), :], sig[x + 1, padded(j), :],
                    beside(sig, (x + 2,), j, 1), beside(sig, (x + 2,), j, -1),
                    along(here, 1), along(here, -1))
                diagonal = jnp.full((ROWS, Z), MASS, jnp.float32)
                for i, side in enumerate(sides):
                    w = 0.5 * (here + side)
                    weights[i, x + 1, plain(j), :] = w
                    diagonal = diagonal + w
                weights[6, x + 1, plain(j), :] = diagonal
            return carry

        lax.fori_loop(0, tiles, step, 0, unroll=4)

    def operate(field, s, low, high, keep):
        def step(j, dots):
            for x in range(low, high):
                d = field[s, x + 2, padded(j), :]
                sides = (
                    field[s, x + 3, padded(j), :], field[s, x + 1, padded(j), :],
                    beside(field, (s, x + 2), j, 1), beside(field, (s, x + 2), j, -1),
                    along(d, 1), along(d, -1))
                total = weights[6, x + 1, plain(j), :] * d
                for i, side in enumerate(sides):
                    total = total - weights[i, x + 1, plain(j), :] * side
                if 0 <= x < X:
                    dots = dots + d * total
                if x < 0:
                    total = jnp.where(has_left, total, 0.0)
                if x >= X:
                    total = jnp.where(has_right, total, 0.0)
                if keep:
                    img[s, x + 1, padded(j), :] = total
            return dots

        return lax.fori_loop(0, tiles, step, zero, unroll=4)

    def complete(it, s, x, j):
        total = part[it, s, x + 1, plain(j), :] if -1 <= x <= X else None
        if x < 1:
            there = from_left[it, s, x + 2, plain(j), :]
            if total is not None:
                there = total + there
            total = jnp.where(has_left, there, 0.0 if x < 0 else total)
        if x > X - 2:
            there = from_right[it, s, x - X + 1, plain(j), :]
            if total is not None:
                there = total + there
            total = jnp.where(has_right, there, 0.0 if x >= X else total)
        return total

    def set_first(s):
        def step(j, carry):
            for x in range(-2, X + 2):
                first_dir[s, x + 2, padded(j), :] = complete(0, s, x, j)
            return carry

        lax.fori_loop(0, tiles, step, 0, unroll=4)

    def set_next(s, size, growth):
        def step(j, carry):
            for x in range(-1, X + 1):
                d = first_dir[s, x + 2, padded(j), :]
                next_dir[s, x + 2, padded(j), :] = (
                    (d - size * complete(1, s, x, j)) + growth * d)
            return carry

        lax.fori_loop(0, tiles, step, 0, unroll=4)

    def face_terms(field, s, factor, into, add):
        def step(j, carry):
            for x in range(X):
                f, a = fwd[s, x + 1, padded(j), :], field[s, x + 2, padded(j), :]
                sides = [
                    (r[s, x + at + 1, padded(j), :], r[s, x + at - 1, padded(j), :],
                     beside(r, (s, x + at), j, 1), beside(r, (s, x + at), j, -1),
                     along(v, 1), along(v, -1))
                    for r, v, at in ((fwd, f, 1), (field, a, 2))
                ]
                sums = None
                for fs, as_ in zip(*sides):
                    term = (f - fs) * (a - as_)
                    sums = term if sums is None else sums + term
                term = factor * sums
                if add:
                    term = term + into[x, plain(j), :]
                into[x, plain(j), :] = term
            return carry

        lax.fori_loop(0, tiles, step, 0, unroll=4)

    def add_electrodes(s):
        at = lax.broadcasted_iota(jnp.int32, (ROWS, Z), 0) * Z + lane
        plus = elec[s, 0] - me * (X * H * Z)
        minus = elec[s, 1] - me * (X * H * Z)

        def step(j, carry):
            for x in range(X):
                here = at + (x * H + ROWS * j) * Z
                v = res[s, x + 1, padded(j), :]
                v = v + jnp.where(here == plus, CURRENT, 0.0)
                v = v - jnp.where(here == minus, CURRENT, 0.0)
                res[s, x + 1, padded(j), :] = v
            return carry

        lax.fori_loop(0, tiles, step, 0, unroll=4)

    scale = []
    for s in range(S):
        w = jnp.float32(0.0)
        for i in range(lines.shape[0]):
            w = w + jnp.where(assign[s] == i, lines[i], 0.0)
        scale.append(-0.5 * w)

    for s in range(S):
        load_misfit[s].wait()
        add_electrodes(s)
        res_halo[s].start()
    sig_halo.start()
    fwd_halo[0].start()
    for copy in load_coef:
        copy.wait()

    for s in range(S):
        res_halo[s].arrive()
        squares, _ = precondition(res, 0, s)
        sum_start(s, squares)
        part_halo[0][s].start()
        if s == 0:
            load_sigma.wait()
            sig_halo.arrive()
            find_weights()

    fwd_halo[1].start()
    align, size = [], []
    for s in range(S):
        part_halo[0][s].arrive()
        set_first(s)
        sum_start(S + s, operate(first_dir, s, -1, X + 1, True))
        sum_start(2 * S + s, *precondition(img, 1, s))
        part_halo[1][s].start()

    for s in range(S):
        align.append(sum_finish(s))
        size.append(align[s] / sum_finish(S + s))
    for s in range(S):
        load_fwd[s].wait()
        fwd_halo[s].arrive()
        face_terms(first_dir, s, scale[s] * size[s], gsum, s > 0)

    for s in range(S):
        part_halo[1][s].arrive()
        squares, cross = sum_finish(2 * S + s, 2)
        now = align[s] - size[s] * (2.0 * cross - size[s] * squares)
        set_next(s, size[s], now / align[s])
        align[s] = now
        sum_start(3 * S + s, operate(next_dir, s, 0, X, False))
    for s in range(S):
        face_terms(next_dir, s, scale[s], gpart.at[s], False)

    last_size = [align[s] / sum_finish(3 * S + s) for s in range(S)]

    def combine(j, carry):
        for x in range(X):
            total = gsum[x, plain(j), :]
            for s in range(S):
                total = total + last_size[s] * gpart[s, x, plain(j), :]
            gsum[x, plain(j), :] = total
        return carry

    lax.fori_loop(0, tiles, combine, 0, unroll=4)

    count = H // nsrc

    def share(t):
        return pl.ds(pl.multiple_of(count * t, count), count)

    give = []
    for k in range(1, nsrc):
        to = lax.rem(mine + k, nsrc)
        give.append(pltpu.make_async_remote_copy(
            gsum.at[:, share(to), :], grecv.at[k - 1], grad_send.at[k], grad_recv.at[k],
            device_id={"src": to}, device_id_type=MESH))
        give[-1].start()

    save = []
    for s in range(S):

        def add_up(j, carry, s=s):
            for x in range(X):
                out[s, x, plain(j), :] = (
                    size[s] * first_dir[s, x + 2, padded(j), :]
                    + last_size[s] * next_dir[s, x + 2, padded(j), :])
            return carry

        lax.fori_loop(0, tiles, add_up, 0, unroll=4)
        save.append(pltpu.make_async_copy(out.at[s], adj_hbm.at[s], out_sem.at[s]))
        save[s].start()

    total = gsum[:, share(mine), :]
    for k in range(1, nsrc):
        give[k - 1].wait()
        total = total + grecv[k - 1]
    gout[...] = total
    last = pltpu.make_async_copy(gout, grad_hbm, out_sem.at[S])
    last.start()

    for s in range(S):
        res_halo[s].leave()
        part_halo[0][s].leave()
        part_halo[1][s].leave()
        fwd_halo[s].leave()
        save[s].wait()
    sig_halo.leave()
    last.wait()


def body(n, nsrc, conductivity, inverse_coefficients, forward_potential, misfit_field,
         electrodes, assignment, line_weight):
    S, X, H, Z = misfit_field.shape
    f32 = jnp.float32
    tall = H + 2 * PAD
    field = pltpu.VMEM((S, X + 2, tall, Z), f32)
    wide = pltpu.VMEM((S, X + 4, tall, Z), f32)
    dma = pltpu.SemaphoreType.DMA
    smem = pl.BlockSpec(memory_space=pltpu.SMEM)
    anywhere = pl.BlockSpec(memory_space=pl.ANY)
    shapes = (
        jax.ShapeDtypeStruct((S, X, H, Z), f32),
        jax.ShapeDtypeStruct((X, H // nsrc, Z), f32),
    )
    results = pl.pallas_call(
        functools.partial(kernel, (n, nsrc, S, X, H, Z)),
        out_shape=shapes,
        in_specs=[smem] * 3 + [anywhere] * 4,
        out_specs=(anywhere, anywhere),
        scratch_shapes=[
            pltpu.VMEM((27, X, H, Z), f32),
            pltpu.VMEM((X + 4, tall, Z), f32),
            pltpu.VMEM((7, X + 2, H, Z), f32),
            field, field, field, wide, wide,
            pltpu.VMEM((S, X, H, Z), f32),
            pltpu.VMEM((3, X + 2, tall, Z), f32),
            pltpu.VMEM((ITERS, S, X + 2, H, Z), f32),
            pltpu.VMEM((ITERS, S, 3, H, Z), f32),
            pltpu.VMEM((ITERS, S, 3, H, Z), f32),
            pltpu.VMEM((X, H, Z), f32),
            pltpu.VMEM((S, X, H, Z), f32),
            pltpu.VMEM((S, X, H, Z), f32),
            pltpu.VMEM((nsrc - 1, X, H // nsrc, Z), f32),
            pltpu.VMEM((X, H // nsrc, Z), f32),
            pltpu.VMEM((4 * S, 2, ROWS, LANES), f32),
            pltpu.VMEM((4 * S, n, 2, ROWS, LANES), f32),
            dma((2 * S + 1 + CHUNKS,)),
            dma((S + 1,)),
            dma((4 * S + 1, 2)),
            dma((4 * S + 1, 2)),
            dma((4 * S, n)),
            dma((4 * S, n)),
            dma((nsrc,)),
            dma((nsrc,)),
        ],
        compiler_params=pltpu.CompilerParams(
            collective_id=0, has_side_effects=True, vmem_limit_bytes=60 * 1024 * 1024),
    )(electrodes, assignment, line_weight, conductivity, inverse_coefficients,
      forward_potential, misfit_field)
    return pl.pallas_call(
        hand_over,
        out_shape=shapes,
        in_specs=[pl.BlockSpec(memory_space=pltpu.VMEM)] * 2,
        out_specs=(pl.BlockSpec(memory_space=pltpu.VMEM),) * 2,
    )(*results)


def hand_over(adj, grad, adj_out, grad_out):
    adj_out[...] = adj[...]
    grad_out[...] = grad[...]


def solution(mesh):
    in_specs = (
        P(("groups", "space"), None, None),
        P(None, ("groups", "space"), None, None),
        P(("groups", "src"), "space", None, None),
        P(("groups", "src"), "space", None, None),
        P(("groups", "src"), None),
        P(("groups", "src")),
        P("groups"),
    )
    out_specs = (P(("groups", "src"), "space", None, None), P(("groups", "space"), "src", None))
    run = functools.partial(body, mesh.shape["space"], mesh.shape["src"])
    return jax.shard_map(run, mesh=mesh, in_specs=in_specs, out_specs=out_specs, check_vma=False)
```
